32 devices in a mesh: groups: 2 (over x), pb: 8 (over z, y), ka: 2 (over core).
Axes of the slice: x: 2, y: 2, z: 4, core: 2. Of those that a mesh axis runs over, the one named last changes fastest.
Arguments:
- surface: float32 [2048, 192], P(('groups', 'pb', 'ka')), parts along dimension 0, may hold values from -6 to 6
- surface_count: int32 [32], P(('groups', 'pb', 'ka')), parts along dimension 0, may hold values from 16 to 64, as said below
- volume: float32 [8192, 192], P(('groups', 'pb', 'ka')), parts along dimension 0, may hold values from -6 to 6
- volume_count: int32 [32], P(('groups', 'pb', 'ka')), parts along dimension 0, may hold values from 64 to 256, as said below
- self_weights: float32 [1, 2, 192, 576], replicated
- self_output: float32 [1, 2, 192, 192], replicated, may hold values from -0.4375 to 0.4375
- cross_query: float32 [1, 2, 192, 192], replicated, may hold values from -0.4375 to 0.4375
- cross_pairs: float32 [1, 2, 192, 384], replicated, may hold values from -0.4375 to 0.4375
- cross_output: float32 [1, 2, 192, 192], replicated, may hold values from -0.4375 to 0.4375
Outputs:
- surface_out: float32 [2048, 192], P(('groups', 'pb', 'ka')), parts along dimension 0
- volume_out: float32 [8192, 192], P(('groups', 'pb', 'ka')), parts along dimension 0
The draws below stay inside these ranges and needn't reach their ends.
There are 2 independent parts, one for each index of `groups`. The reference program is written for one: setup_inputs(seed, part) draws one part's arguments, and reference() takes and returns one part's arrays. A program takes and returns all parts, laid end to end along the dimension named above; an argument that names none is the same for every part. Nothing has to cross between parts.
Inputs may be any that keep to these rules, and one draw needn't show every extreme that they name: surface_count[i] is the number of live slots of surface shard i; live slots come first in the shard; in every draw some shard is full. volume_count[i] is the number of live slots of volume shard i; live slots come first in the shard; in every draw some shard is full.
All inputs are finite; a program needn't handle non-finite values.
Results may differ from the reference program's by a relative error of at most 0.0003.
Values sent between devices are 32-bit elements; how exact they have to be, the bound alone decides.
A program may use at most 128 MiB of HBM per device.

```python
import jax
import jax.numpy as jnp
from jax import lax

D = 192
HEADS = 3
HEAD_DIM = 64
BLOCKS = 1
SURF_DEV = 64
VOL_DEV = 256
SHARDS = 16


def shard_counts(key, capacity):
    first_key, second = jax.random.split(key)
    counts = jax.random.randint(first_key, (SHARDS,), max(1, capacity // 4), capacity + 1)
    full_slot = jax.random.randint(second, (), 0, SHARDS)
    return jnp.where(jnp.arange(SHARDS) == full_slot, capacity, counts).astype(jnp.int32)


def draw_surface_count(key, part):
    return shard_counts(jax.random.fold_in(key, 11), SURF_DEV)


def draw_volume_count(key, part):
    return shard_counts(jax.random.fold_in(key, 12), VOL_DEV)


def draw_self_weights(key, part):
    drawn = jax.random.normal(jax.random.fold_in(key, 13), (BLOCKS, 2, D, 3 * D), jnp.float32) * D ** (-0.5)
    return drawn


def block_scale(own_key, shape, cuts, least, top_value):
    gain, own = 1.0, jax.random.fold_in(own_key, 6)
    for axis_at, parts in cuts:
        draws = jnp.exp(jax.random.uniform(jax.random.fold_in(own, axis_at), (parts,), jnp.float32, least / len(cuts), top_value / len(cuts)))
        gain = gain * jnp.repeat(draws, shape[axis_at] // parts).reshape([-1 if axis == axis_at else 1 for axis in range(len(shape))])
    return gain


def noise(key, dims, scale, bound, cuts=(), kind=jnp.bfloat16):
    entries = jax.random.normal(key, dims, jnp.float32) * scale
    if len(cuts) > 0:
        entries = block_scale(key, dims, cuts, -0.22, 0.18) * entries
    return jnp.clip(entries, min=-bound, max=bound).astype(kind)


def setup_inputs(seed: int = 0, part: int = 0) -> dict:
    keys = jax.random.split(jax.random.key(seed), 10)
    own_keys = jax.random.split(jax.random.fold_in(keys[9], part), 10)
    return {
        "surface": noise(own_keys[0], (SURF_DEV * SHARDS, D), 1.0, 6.0, ((0, 16),), jnp.float32),
        "surface_count": draw_surface_count(jax.random.fold_in(jax.random.fold_in(keys[9], part), 71), part),
        "volume": noise(own_keys[2], (VOL_DEV * SHARDS, D), 1.0, 6.0, ((0, 16),), jnp.float32),
        "volume_count": draw_volume_count(jax.random.fold_in(jax.random.fold_in(keys[9], part), 71), part),
        "self_weights": draw_self_weights(jax.random.fold_in(keys[9], 71), part),
        "self_output": noise(keys[5], (BLOCKS, 2, D, D), D ** -0.5, 0.4375, (), jnp.float32),
        "cross_query": noise(keys[6], (BLOCKS, 2, D, D), D ** -0.5, 0.4375, (), jnp.float32),
        "cross_pairs": noise(keys[7], (BLOCKS, 2, D, 2 * D), D ** -0.5, 0.4375, (), jnp.float32),
        "cross_output": noise(keys[8], (BLOCKS, 2, D, D), D ** -0.5, 0.4375, (), jnp.float32),
    }


HIGH = lax.Precision.HIGHEST

def layer_norm(values):
    center = values - lax.optimization_barrier(jnp.mean(values, axis=-1, keepdims=True))
    spread = lax.optimization_barrier(jnp.mean(center * center, axis=-1, keepdims=True))
    return center * lax.rsqrt(spread + 1e-05)

def live_rows(counts, capacity):
    slot_index = jnp.arange(capacity, dtype=jnp.int32)
    return (slot_index[None, :] < counts.astype(jnp.int32)[:, None]).reshape(-1)

def attention(queries, key_rows, value_rows, key_live):
    row_total = queries.shape[0]
    block_rows = 256 if row_total % 256 == 0 else row_total
    blocks = queries.reshape(row_total // block_rows, block_rows, HEADS, HEAD_DIM)

    def one_block(query_block):
        scores = jnp.einsum('qhe,khe->hqk', query_block, key_rows, precision=HIGH)
        scores = jnp.where(key_live[None, None, :], scores, -1e+30)
        row_max = lax.optimization_barrier(jnp.max(scores, axis=-1, keepdims=True))
        weights = jnp.where(key_live[None, None, :], jnp.exp(scores - row_max), 0.0)
        row_sum = lax.optimization_barrier(jnp.sum(weights, axis=-1))
        attended = jnp.einsum('hqk,khe->qhe', weights, value_rows, precision=HIGH)
        return attended / jnp.transpose(row_sum)[:, :, None]
    return lax.map(one_block, blocks).reshape(row_total, D)

def attend(query_normed, w_query, key_normed, w_pair, key_live, w_output):
    queries = jnp.dot(query_normed, w_query, precision=HIGH) * HEAD_DIM ** (-0.5)
    key_value = jnp.dot(key_normed, w_pair, precision=HIGH)
    key_rows = key_value[:, :D].reshape(-1, HEADS, HEAD_DIM)
    value_rows = key_value[:, D:].reshape(-1, HEADS, HEAD_DIM)
    attended = attention(queries.reshape(-1, HEADS, HEAD_DIM), key_rows, value_rows, key_live)
    return jnp.dot(attended, w_output, precision=HIGH)

def reference(surface, surface_count, volume, volume_count, self_weights, self_output, cross_query, cross_pairs, cross_output):
    surf_live = live_rows(surface_count, SURF_DEV)
    vol_live = live_rows(volume_count, VOL_DEV)
    for block_index in range(BLOCKS):
        surf_norm = layer_norm(surface)
        vol_norm = layer_norm(volume)
        surf_weights = self_weights[block_index, 0]
        vol_weights = self_weights[block_index, 1]
        surf_next = surface + attend(surf_norm, surf_weights[:, :D], surf_norm, surf_weights[:, D:], surf_live, self_output[block_index, 0])
        vol_next = volume + attend(vol_norm, vol_weights[:, :D], vol_norm, vol_weights[:, D:], vol_live, self_output[block_index, 1])
        surf_norm = layer_norm(surf_next)
        vol_norm = layer_norm(vol_next)
        surface = surf_next + attend(surf_norm, cross_query[block_index, 0], vol_norm, cross_pairs[block_index, 0], vol_live, cross_output[block_index, 0])
        volume = vol_next + attend(vol_norm, cross_query[block_index, 1], surf_norm, cross_pairs[block_index, 1], surf_live, cross_output[block_index, 1])
    surface_out = jnp.where(surf_live[:, None], surface, 0.0)
    volume_out = jnp.where(vol_live[:, None], volume, 0.0)
    return (surface_out, volume_out)
```

```python
import functools
import math

import jax
import jax.numpy as jnp
from jax import lax
from jax.experimental import pallas as pl
from jax.experimental.pallas import tpu as pltpu
from jax.sharding import PartitionSpec as P

HEADS = 3
LANES = 128
PART = 256
DEAD = -(2.0 ** 100)
LOW = -1e30
HIGH = lax.Precision.HIGHEST
MESH = pl.DeviceIdType.MESH
F32 = jnp.float32
BF16 = jnp.bfloat16


def layer_norm(values):
    center = values - jnp.mean(values, axis=-1, keepdims=True)
    spread = jnp.mean(center * center, axis=-1, keepdims=True)
    return center * lax.rsqrt(spread + 1e-05)


def split(values):
    high = values.astype(BF16)
    return high, (values - high.astype(F32)).astype(BF16)


def dot(a, b, dims=((1,), (0,))):
    return lax.dot_general(a, b, (dims, ((), ())), precision=HIGH, preferred_element_type=F32)


def bdot(a, b):
    return jnp.dot(a, b, preferred_element_type=F32)


def pack(rows):
    total = rows.shape[0]
    tail = rows[:, LANES:]
    half = total // 2
    return jnp.concatenate([rows[:, :LANES], jnp.concatenate([tail[:half], tail[half:]], axis=1)], axis=0)


def unpack(first, second, dead):
    tail = jnp.concatenate([second, pltpu.roll(second, LANES // 2, 1)], axis=0)
    lane = lax.broadcasted_iota(jnp.int32, tail.shape, 1)
    tail = jnp.where(lane < LANES // 2, tail, jnp.where(lane == LANES // 2, dead, 0.0))
    return jnp.concatenate([first, tail], axis=1)


def head_mask(rows, width, head):
    column = lax.broadcasted_iota(jnp.int32, (rows, width), 1)
    size = width // HEADS
    return (column >= head * size) & (column < (head + 1) * size)


def kernel(
    n,
    surf_ref, scount_ref, vol_ref, vcount_ref, sw_ref, so_ref, cq_ref, cp_ref, co_ref,
    surf_out, vol_out,
    buf, xcat_v, xt_v, xcat_s, xt_s, q_v, q_s, acc_v, acc_s, stat_v, stat_s,
    right_send, right_recv, left_send, left_recv, sib_send, sib_recv,
):
    S, D = surf_ref.shape
    V = vol_ref.shape[0]
    half = n // 2
    pack_v = V // 2 + V // 4
    pack_s = S + S // 2
    chunk = ((0, pack_v + pack_s + 8), (pack_v + pack_s + 8, pack_v))
    chunk0 = chunk[1][0]

    pb = lax.axis_index("pb")
    ka = lax.axis_index("ka")
    grp = lax.axis_index("groups")

    def to_place(i):
        return (1 - i % 2) * (i // 2) + (i % 2) * (n - 1 - i // 2)

    def to_index(p):
        h = p // half
        return (1 - h) * (2 * p) + h * (2 * (n - 1 - p) + 1)

    place = to_place(pb)
    right = (grp, to_index((place + 1) % n), ka)
    left = (grp, to_index((place + n - 1) % n), ka)
    sibling = (grp, pb, 1 - ka)

    barrier = pltpu.get_barrier_semaphore()
    for other in (left, right, sibling):
        pl.semaphore_signal(barrier, inc=1, device_id=other, device_id_type=MESH)

    def ring(phase, rightward, source, target, c, step):
        start, size = chunk[c]
        sems = (right_send, right_recv) if rightward else (left_send, left_recv)
        return pltpu.make_async_remote_copy(
            src_ref=buf.at[phase, 0, source, pl.ds(start, size)],
            dst_ref=buf.at[phase, 0, target, pl.ds(start, size)],
            send_sem=sems[0].at[phase, step, c],
            recv_sem=sems[1].at[phase, step, c],
            device_id=right if rightward else left,
            device_id_type=MESH,
        )

    def share(phase, slot):
        return pltpu.make_async_remote_copy(
            src_ref=buf.at[phase, 0, slot],
            dst_ref=buf.at[phase, 1, slot],
            send_sem=sib_send.at[phase, slot],
            recv_sem=sib_recv.at[phase, slot],
            device_id=sibling,
            device_id_type=MESH,
        )

    row8 = lax.broadcasted_iota(jnp.int32, (8, LANES), 0)
    counts = jnp.where(row8 < 4, scount_ref[0].astype(F32), vcount_ref[0].astype(F32))

    def publish(phase, surf_norm, vol_norm):
        buf[phase, 0, 0, pl.ds(0, pack_v), :] = pack(vol_norm[: V // 2])
        buf[phase, 0, 0, pl.ds(pack_v, pack_s), :] = pack(surf_norm)
        buf[phase, 0, 0, pl.ds(pack_v + pack_s, 8), :] = counts
        buf[phase, 0, 0, pl.ds(chunk0, pack_v), :] = pack(vol_norm[V // 2:])
        if phase == 0:
            pl.semaphore_wait(barrier, 3)
        for c in range(2):
            ring(phase, True, 0, 1, c, 0).start()
            ring(phase, False, 0, 2, c, 0).start()
        share(phase, 0).start()

    def queries(q_ref, normed, w_query, w_key):
        rows = normed.shape[0]
        q = dot(normed, w_query) * ((D // HEADS) ** -0.5 * math.log2(math.e))
        stacked = jnp.concatenate(
            [jnp.where(head_mask(rows, D, h), q, 0.0) for h in range(HEADS)], axis=0
        )
        wide = dot(w_key, stacked, ((1,), (1,)))
        high, low = split(wide)
        row = lax.broadcasted_iota(jnp.int32, (PART - D, HEADS * rows), 0)
        one = jnp.where(row == 0, 1.0, 0.0).astype(BF16)
        zero = jnp.zeros((PART - D, HEADS * rows), BF16)
        q_ref[pl.ds(0, PART), :] = jnp.concatenate([high, one], axis=0)
        q_ref[pl.ds(PART, PART), :] = jnp.concatenate([high, zero], axis=0)
        q_ref[pl.ds(2 * PART, PART), :] = jnp.concatenate([low, zero], axis=0)

    def keys(phase, slot, side):
        def put(x, cat, xt, base):
            rows = x.shape[0]
            high, low = split(x)
            cat[pl.ds(base, rows), pl.ds(0, PART)] = high
            cat[pl.ds(base, rows), pl.ds(PART, PART)] = low
            cat[pl.ds(base, rows), pl.ds(2 * PART, PART)] = high

        def flip(x, xt, base):
            rows = x.shape[0]
            turned = jnp.transpose(x)[:D]
            high, low = split(turned)
            xt[pl.ds(0, D), pl.ds(base, rows)] = high
            xt[pl.ds(D, D), pl.ds(base, rows)] = low

        def block(start, rows, line, first_row):
            first = buf[phase, side, slot, pl.ds(start, rows), :]
            second = buf[phase, side, slot, pl.ds(start + rows, rows // 2), :]
            limit = buf[phase, side, slot, pl.ds(pack_v + pack_s + line, 1), :]
            index = lax.broadcasted_iota(jnp.int32, (rows, LANES), 0).astype(F32) + first_row
            return unpack(first, second, jnp.where(index < limit, 0.0, DEAD))

        for c in range(2):
            x = block(chunk[c][0], V // 2, 4, float(c * (V // 2)))
            put(x, xcat_v, xt_v, side * V + c * (V // 2))
            flip(x, xt_v, side * V + c * (V // 2))
        x = block(pack_v, S, 0, 0.0)
        put(x, xcat_s, xt_s, side * S)
        return x

    def update(cat, xt, q_ref, acc, stat, width):
        total = q_ref.shape[1]
        for at in range(0, total, width):
            cols = pl.ds(at, width)
            s = bdot(cat[...], q_ref[:, cols])
            old = stat[pl.ds(0, 1), cols]
            new = jnp.maximum(old, jnp.max(s, axis=0, keepdims=True))
            w = jnp.exp2(s - new)
            scale = jnp.exp2(old - new)
            stat[pl.ds(0, 1), cols] = new
            stat[pl.ds(8, 1), cols] = stat[pl.ds(8, 1), cols] * scale + jnp.sum(w, axis=0, keepdims=True)
            high, low = split(w)
            both = bdot(xt[...], high)
            more = bdot(xt[pl.ds(0, D), :], low)
            acc[:, cols] = acc[:, cols] * scale + (both[:D] + both[D:] + more)

    def compute(phase, slot):
        surf = [keys(phase, slot, side) for side in range(2)]
        turned = jnp.transpose(jnp.concatenate(surf, axis=0))[:D]
        high, low = split(turned)
        xt_s[pl.ds(0, D), :] = high
        xt_s[pl.ds(D, D), :] = low
        if phase == 0:
            update(xcat_v, xt_v, q_v, acc_v, stat_v, V)
            update(xcat_s, xt_s, q_s, acc_s, stat_s, HEADS * S)
        else:
            update(xcat_v, xt_v, q_s, acc_s, stat_s, HEADS * S)
            update(xcat_s, xt_s, q_v, acc_v, stat_v, V)

    def clear():
        for acc, stat in ((acc_v, stat_v), (acc_s, stat_s)):
            acc[...] = jnp.zeros_like(acc)
            stat[pl.ds(0, 8), :] = jnp.full((8, stat.shape[1]), LOW, F32)
            stat[pl.ds(8, 8), :] = jnp.zeros((8, stat.shape[1]), F32)

    def finish(acc, stat, w_value, w_out):
        rows = acc.shape[1] // HEADS
        normal = acc[...] / stat[pl.ds(8, 1), :]
        wide = dot(jnp.transpose(normal), w_value)
        attended = sum(
            jnp.where(head_mask(rows, D, h), wide[h * rows:(h + 1) * rows], 0.0) for h in range(HEADS)
        )
        return dot(attended, w_out)

    def gather(phase):
        def step(d, carry):
            for c in range(2):
                def take_left():
                    ring(phase, True, 0, 2 * d - 1, c, d - 1).wait_recv()

                def take_right():
                    ring(phase, False, 0, jnp.minimum(2 * d, n - 1), c, d - 1).wait_recv()

                @pl.when(d < half)
                def _():
                    take_left()
                    take_right()

                    @pl.when(d < half - 1)
                    def _():
                        ring(phase, True, 2 * d - 1, 2 * d + 1, c, d).start()
                        ring(phase, False, 2 * d, 2 * d + 2, c, d).start()

                    @pl.when(d == half - 1)
                    def _():
                        if c == 0:
                            ring(phase, True, n - 3, n - 1, c, half - 1).start()
                        else:
                            ring(phase, False, n - 2, n - 1, c, half - 1).start()

                    if c == 1:
                        share(phase, 2 * d - 1).start()
                        share(phase, 2 * d).start()

                @pl.when(d == half)
                def _():
                    if c == 0:
                        ring(phase, True, 0, n - 1, 0, half - 1).wait_recv()
                        ring(phase, False, 0, n - 1, 1, half - 1).wait_recv()
                        share(phase, n - 1).start()

                if c == 0:
                    @pl.when(d > 1)
                    def _():
                        share(phase, 2 * d - 3).wait_recv()
                        compute(phase, 2 * d - 3)
                else:
                    share(phase, 2 * d - 2).wait_recv()
                    compute(phase, 2 * d - 2)
            return carry

        lax.fori_loop(1, half + 1, step, 0)
        share(phase, n - 1).wait_recv()
        compute(phase, n - 1)

    def drain(phase):
        for d in range(half):
            for c in range(2):
                if d < half - 1 or c == 0:
                    ring(phase, True, 0, 0, c, d).wait_send()
                if d < half - 1 or c == 1:
                    ring(phase, False, 0, 0, c, d).wait_send()
        for slot in range(n):
            share(phase, slot).wait_send()

    surf_norm = layer_norm(surf_ref[...])
    vol_norm = layer_norm(vol_ref[...])
    publish(0, surf_norm, vol_norm)
    ws = sw_ref[0, 0]
    wv = sw_ref[0, 1]
    queries(q_s, surf_norm, ws[:, :D], ws[:, D:2 * D])
    queries(q_v, vol_norm, wv[:, :D], wv[:, D:2 * D])
    clear()
    gather(0)
    surf_next = surf_ref[...] + finish(acc_s, stat_s, sw_ref[0, 0][:, 2 * D:], so_ref[0, 0])
    vol_next = vol_ref[...] + finish(acc_v, stat_v, sw_ref[0, 1][:, 2 * D:], so_ref[0, 1])
    surf_norm = layer_norm(surf_next)
    vol_norm = layer_norm(vol_next)
    publish(1, surf_norm, vol_norm)
    surf_out[...] = surf_next
    vol_out[...] = vol_next
    queries(q_s, surf_norm, cq_ref[0, 0], cp_ref[0, 0][:, :D])
    queries(q_v, vol_norm, cq_ref[0, 1], cp_ref[0, 1][:, :D])
    clear()
    gather(1)
    for out, acc, stat, which, count in (
        (surf_out, acc_s, stat_s, 0, scount_ref), (vol_out, acc_v, stat_v, 1, vcount_ref)
    ):
        value = out[...] + finish(acc, stat, cp_ref[0, which][:, D:], co_ref[0, which])
        row = lax.broadcasted_iota(jnp.int32, value.shape, 0)
        out[...] = jnp.where(row < count[0], value, 0.0)
    drain(0)
    drain(1)


def solution(mesh):
    n = mesh.shape["pb"]

    def local(surface, surface_count, volume, volume_count, *weights):
        S, D = surface.shape
        V = volume.shape[0]
        rows = V + V // 2 + S + S // 2 + 8
        vmem = pl.BlockSpec(memory_space=pltpu.VMEM)
        smem = pl.BlockSpec(memory_space=pltpu.SMEM)
        return pl.pallas_call(
            functools.partial(kernel, n),
            out_shape=(
                jax.ShapeDtypeStruct((S, D), F32),
                jax.ShapeDtypeStruct((V, D), F32),
            ),
            in_specs=[vmem, smem, vmem, smem] + [vmem] * 5,
            out_specs=(vmem, vmem),
            scratch_shapes=[
                pltpu.VMEM((2, 2, n, rows, LANES), F32),
                pltpu.VMEM((2 * V, 3 * PART), BF16),
                pltpu.VMEM((2 * D, 2 * V), BF16),
                pltpu.VMEM((2 * S, 3 * PART), BF16),
                pltpu.VMEM((2 * D, 2 * S), BF16),
                pltpu.VMEM((3 * PART, HEADS * V), BF16),
                pltpu.VMEM((3 * PART, HEADS * S), BF16),
                pltpu.VMEM((D, HEADS * V), F32),
                pltpu.VMEM((D, HEADS * S), F32),
                pltpu.VMEM((16, HEADS * V), F32),
                pltpu.VMEM((16, HEADS * S), F32),
                pltpu.SemaphoreType.DMA((2, n // 2, 2)),
                pltpu.SemaphoreType.DMA((2, n // 2, 2)),
                pltpu.SemaphoreType.DMA((2, n // 2, 2)),
                pltpu.SemaphoreType.DMA((2, n // 2, 2)),
                pltpu.SemaphoreType.DMA((2, n)),
                pltpu.SemaphoreType.DMA((2, n)),
            ],
            compiler_params=pltpu.CompilerParams(
                collective_id=0, has_side_effects=True, vmem_limit_bytes=48 * 2 ** 20
            ),
        )(surface, surface_count, volume, volume_count, *weights)

    rows = P(("groups", "pb", "ka"), None)
    count = P(("groups", "pb", "ka"))
    return jax.shard_map(
        local,
        mesh=mesh,
        in_specs=(rows, count, rows, count) + (P(),) * 5,
        out_specs=(rows, rows),
        check_vma=False,
    )
```
